512 devices in a mesh: blk: 32 (over y, x), col: 16 (over z, core).
Axes of the slice: x: 4, y: 8, z: 8, core: 2. Of those that a mesh axis runs over, the one named last changes fastest.
Arguments:
- pair_occ: int32 [32, 256], P('blk', 'col'), may hold values from 0 to 3
- pair_offset: int32 [32, 256], P('blk', 'col'), may hold values from 0 to 2, as said below
- pair_other: int32 [32, 256], P('blk', 'col'), may hold values from 0 to 3
- pno_blocks: int32 [32, 256], P('blk', 'col'), may hold values from 1 to 4
- pno_coef: float32 [128, 128, 1024], P('blk'), may hold values from -0.5 to 0.5
- amplitudes: float32 [32, 256, 128, 128], P('blk', 'col'), may hold values from -0.4 to 0.4
- integrals: float32 [32, 256, 128, 128], P('blk', 'col'), may hold values from -0.5 to 0.5
Outputs:
- density: float32 [32, 1024, 1024], P('blk', None, 'col')
The draws below stay inside these ranges and needn't reach their ends.
Inputs may be any that keep to these rules, and one draw needn't show every extreme that they name: `pair_offset`: in every device's 16 slots the first three name the offsets 0, 1 and 2 in order.
All inputs are finite; a program needn't handle non-finite values.
Results may differ from the reference program's by a relative error of at most 0.0003.
Values sent between devices are 32-bit elements; how exact they have to be, the bound alone decides.
No kernel may reach another device: no remote copies, remote signals or barrier semaphores. Data moves between devices by JAX's collectives and lax.ppermute only.
A program may use at most 64 MiB of HBM per device.

```python
import jax
import jax.numpy as jnp
from jax import lax

P_SIZE = 128
ORB = 4
NPAIR = 16
NAO = 1024
PAIRS = 256
NORB = 128
BLOCK = 32
N_BLK = 32


def draw_pair_offset(key, part):
    key = jax.random.fold_in(key, 7)
    random_offsets = jax.random.randint(key, (N_BLK, PAIRS), 0, 3, dtype=jnp.int32)
    slot_number = lax.broadcasted_iota(jnp.int32, (N_BLK, PAIRS), 1) % NPAIR
    return jnp.where(slot_number < 3, slot_number, random_offsets).astype(jnp.int32)


def plant(array, own_key, smallest, high):
    place = [jax.random.randint(jax.random.fold_in(own_key, axis), (), 0, length) for axis, length in enumerate(array.shape)]
    longest = array.shape.index(max(array.shape))
    next_to = place[:longest] + [(place[longest] + 1) % array.shape[longest]] + place[longest + 1:]
    return array.at[tuple(place)].set(smallest).at[tuple(next_to)].set(high)


def level_of(stream_key, extent, cuts, least, top_value):
    def one(dim, blocks):
        steps = jax.random.uniform(jax.random.fold_in(jax.random.fold_in(stream_key, 6), dim), (blocks,), jnp.float32, least / len(cuts), top_value / len(cuts))
        return jnp.repeat(jnp.exp(steps), extent[dim] // blocks).reshape((-1,) + (1,) * (len(extent) - dim - 1))

    level = one(*cuts[0])
    for cut in cuts[1:]:
        level = level * one(*cut)
    return level


def centred(stream_key, dims, width, most, cuts=(), held_as=jnp.bfloat16):
    values = width * jax.random.normal(stream_key, dims, jnp.float32)
    if cuts:
        values = values * level_of(stream_key, dims, cuts, -0.22, 0.18)
    return jnp.clip(values, -most, most).astype(held_as)


def setup_inputs(seed: int = 0) -> dict:
    arg_keys = jax.random.split(jax.random.key(seed), 8)
    pair_occ = plant(jax.random.randint(arg_keys[0], (N_BLK, PAIRS), 0, ORB), jax.random.fold_in(arg_keys[0], 1), 0, ORB - 1).astype(jnp.int32)
    pair_offset = draw_pair_offset(jax.random.fold_in(arg_keys[7], 71), 0)
    pair_other = plant(jax.random.randint(arg_keys[2], (N_BLK, PAIRS), 0, ORB), jax.random.fold_in(arg_keys[2], 1), 0, ORB - 1).astype(jnp.int32)
    pno_blocks = plant(jax.random.randint(arg_keys[3], (N_BLK, PAIRS), 1, 5), jax.random.fold_in(arg_keys[3], 1), 1, 4).astype(jnp.int32)
    pno_coef = centred(arg_keys[4], (NORB, P_SIZE, NAO), P_SIZE ** -0.5, 0.5, ((0, 32),), jnp.float32)
    amplitudes = centred(arg_keys[5], (N_BLK, PAIRS, P_SIZE, P_SIZE), 0.06, 0.4, ((0, 32), (1, 16)), jnp.float32)
    integrals = centred(arg_keys[6], (N_BLK, PAIRS, P_SIZE, P_SIZE), P_SIZE ** -0.5, 0.5, ((0, 32), (1, 16)), jnp.float32)
    return {"pair_occ": pair_occ, "pair_offset": pair_offset, "pair_other": pair_other, "pno_blocks": pno_blocks, "pno_coef": pno_coef, "amplitudes": amplitudes, "integrals": integrals}


def tile_density(extended, coefficients, occ, offset, other, blocks, amps, ints):
    levels = lax.broadcasted_iota(jnp.int32, (occ.shape[0], P_SIZE), 1)
    pno_keep = (levels < BLOCK * blocks[:, None]).astype(jnp.float32)
    masked = amps * pno_keep[:, :, None] * pno_keep[:, None, :]
    lagrangian = jnp.einsum("nac,nbc->nab", masked, ints, precision=lax.Precision.HIGHEST)
    slot_index = (offset * ORB + other).astype(jnp.int32)
    partner = jnp.take(extended, slot_index, axis=0)
    images = jnp.einsum("nab,nbk->nak", lagrangian, partner, precision=lax.Precision.HIGHEST)
    owners = (occ[:, None] == jnp.arange(ORB, dtype=jnp.int32)[None, :]).astype(jnp.float32)
    collected = jnp.einsum("no,nak->oak", owners, images, precision=lax.Precision.HIGHEST)
    stacked = collected.reshape(ORB * P_SIZE, NAO)
    flat_coef = coefficients.reshape(ORB * P_SIZE, NAO)
    return lax.dot_general(flat_coef, stacked, (((0,), (0,)), ((), ())), precision=lax.Precision.HIGHEST, preferred_element_type=jnp.float32)


def reference(pair_occ, pair_offset, pair_other, pno_blocks, pno_coef, amplitudes, integrals):
    coefficients = pno_coef.reshape(N_BLK, ORB, P_SIZE, NAO)
    extended = jnp.concatenate([jnp.roll(coefficients, 1, 0), coefficients, jnp.roll(coefficients, -1, 0)], axis=1)

    def one_tile(pieces):
        return tile_density(*pieces)

    return lax.map(one_tile, (extended, coefficients, pair_occ, pair_offset, pair_other, pno_blocks, amplitudes, integrals))
```

```python
import jax
import jax.numpy as jnp
from jax import lax
from jax.experimental import pallas as pl
from jax.experimental.pallas import tpu as pltpu
from jax.sharding import PartitionSpec as P

F32 = jnp.float32
BF16 = jnp.bfloat16
ORB = 4
PNO = 128
AO = 1024
SLOTS = 16
CHIPS = 8
WIDE = AO // 2
NARROW = AO // 16
HALF = PNO // 2
ROWS = SLOTS * HALF
META = 8
TILES = 3 * ORB


def split(x):
    hi = x.astype(BF16)
    return hi, (x - hi.astype(F32)).astype(BF16)


def dot(a, b, dims=((1,), (0,))):
    return lax.dot_general(a, b, (dims, ((), ())), preferred_element_type=F32)


def dot3(a, b, dims=((1,), (0,))):
    return dot(a[0], b[0], dims) + (dot(a[0], b[1], dims) + dot(a[1], b[0], dims))


def select_kernel(coef_ref, out_ref):
    core = lax.axis_index("col") % 2
    first = core == 0
    left = lax.broadcasted_iota(jnp.int32, (PNO, 128), 1) < NARROW
    for k in range(CHIPS // 2):
        a = coef_ref[0, :, 256 * k : 256 * k + 128]
        b = coef_ref[0, :, 256 * k + 128 : 256 * k + 256]
        moved = pltpu.roll(jnp.where(first, b, a), NARROW, 1)
        out_ref[:, 128 * k : 128 * k + 128] = jnp.where(
            left, jnp.where(first, a, moved), jnp.where(first, moved, b)
        )


def lagrangian_kernel(occ_ref, offset_ref, other_ref, blocks_ref, amp_ref, int_ref, keep_ref, send_ref):
    upper = (lax.axis_index("col") // 2) % 2 == 1
    rows = lax.broadcasted_iota(jnp.int32, (PNO, PNO), 0)
    cols = lax.broadcasted_iota(jnp.int32, (PNO, PNO), 1)
    far = jnp.maximum(rows, cols)
    lane = lax.broadcasted_iota(jnp.int32, (META, 128), 1)
    meta = jnp.zeros((META, 128), F32)
    for p in range(SLOTS):
        kept = jnp.where(far < PNO // 4 * blocks_ref[0, p], amp_ref[0, p], 0.0)
        lag = dot3(split(kept), split(int_ref[0, p]), ((1,), (1,)))
        low, high = lag[:HALF], lag[HALF:]
        keep_ref[p * HALF : (p + 1) * HALF, :] = jnp.where(upper, high, low)
        send_ref[p * HALF : (p + 1) * HALF, :] = jnp.where(upper, low, high)
        block = (offset_ref[0, p] * ORB + other_ref[0, p]) * ORB + occ_ref[0, p]
        meta = jnp.where(lane == p, block.astype(F32), meta)
    keep_ref[ROWS:, :] = meta
    send_ref[ROWS:, :] = meta


def gather_kernel(m0, m1, m2, m3, l0, l1, l2, l3, x_ref, hi_ref, lo_ref, same_ref, block_ref):
    block_ref[...] = jnp.zeros_like(block_ref)
    for meta_ref, lag_ref in ((m0, l0), (m1, l1), (m2, l2), (m3, l3)):
        for p in range(SLOTS):
            number = meta_ref[0, p].astype(jnp.int32)
            block_ref[number] += lag_ref[p * HALF : (p + 1) * HALF, :]
    for side, first in enumerate((0, 2 * ORB)):
        for j in range(ORB):
            for o in range(ORB):
                hi, lo = split(block_ref[(first + j) * ORB + o])
                at = (slice(o * HALF, (o + 1) * HALF), slice((side * ORB + j) * PNO, (side * ORB + j + 1) * PNO))
                hi_ref[at] = hi
                lo_ref[at] = lo
    total = jnp.zeros((ORB * HALF, WIDE), F32)
    for j in range(ORB):
        lhs = jnp.concatenate([block_ref[(ORB + j) * ORB + o] for o in range(ORB)], axis=0)
        total += dot3(split(lhs), split(x_ref[j * PNO : (j + 1) * PNO, :]))
    same_ref[...] = total


def images_kernel(hi_ref, lo_ref, same_ref, prev_ref, next_ref, out_ref):
    total = same_ref[...]
    for side, x_ref in enumerate((prev_ref, next_ref)):
        x = split(x_ref[...])
        at = slice(side * ORB * PNO, (side + 1) * ORB * PNO)
        total += dot3((hi_ref[:, at], lo_ref[:, at]), x)
    left = lax.broadcasted_iota(jnp.int32, (2 * HALF, 128), 1) < NARROW
    for k in range(CHIPS // 2):
        top = total[: 2 * HALF, 128 * k : 128 * k + 128]
        low = total[2 * HALF :, 128 * k : 128 * k + 128]
        out_ref[2 * k] = jnp.where(left, top, pltpu.roll(low, NARROW, 1))
        out_ref[2 * k + 1] = jnp.where(left, pltpu.roll(top, NARROW, 1), low)


def density_kernel(part_ref, coef_ref, out_ref):
    sums = []
    for h in range(2):
        s = (part_ref[h] + part_ref[h + 2]) + (part_ref[h + 4] + part_ref[h + 6])
        sums.append(s.T)
    total = jnp.zeros((NARROW, AO), F32)
    for pair in range(2):
        lhs = jnp.concatenate([s[NARROW * pair : NARROW * (pair + 1)] for s in sums], axis=1)
        rhs = jnp.concatenate(
            [
                coef_ref[2 * pair + o, HALF * h : HALF * (h + 1), :]
                for h in range(2)
                for o in range(2)
            ],
            axis=0,
        )
        total += dot3(split(lhs), split(rhs))
    out_ref[...] = total


def cost(macs, size):
    return pl.CostEstimate(flops=2 * macs, bytes_accessed=size, transcendentals=0)


PARAMS = pltpu.CompilerParams(vmem_limit_bytes=48 * 1024 * 1024)


def local(pair_occ, pair_offset, pair_other, pno_blocks, pno_coef, amplitudes, integrals):
    smem = pl.BlockSpec(memory_space=pltpu.SMEM)
    tiles = lax.axis_size("blk")
    devices = lax.axis_size("col")

    own = pl.pallas_call(
        select_kernel,
        grid=(ORB,),
        in_specs=[pl.BlockSpec((1, PNO, AO), lambda i: (i, 0, 0))],
        out_specs=pl.BlockSpec((PNO, WIDE), lambda i: (i, 0)),
        out_shape=jax.ShapeDtypeStruct((ORB * PNO, WIDE), F32),
        compiler_params=PARAMS,
        cost_estimate=cost(0, 3 << 20),
        name="select",
    )(pno_coef)
    prev = lax.ppermute(own, "blk", [(i, (i + 1) % tiles) for i in range(tiles)])
    succ = lax.ppermute(own, "blk", [((i + 1) % tiles, i) for i in range(tiles)])

    half = jax.ShapeDtypeStruct((ROWS + META, 128), F32)
    keep, send = pl.pallas_call(
        lagrangian_kernel,
        in_specs=[smem] * 4 + [pl.BlockSpec(memory_space=pltpu.VMEM)] * 2,
        out_shape=(half, half),
        compiler_params=PARAMS,
        cost_estimate=cost(3 * SLOTS * PNO**3, 3 << 20),
        name="lagrangian",
    )(pair_occ, pair_offset, pair_other, pno_blocks, amplitudes, integrals)

    swap = lambda x, bit: lax.ppermute(x, "col", [(i, i ^ bit) for i in range(devices)])
    far = swap(send, 2)
    halves = (keep, far, swap(keep, 1), swap(far, 1))
    meta = pl.BlockSpec((META, 128), lambda i: (ROWS // META, 0), memory_space=pltpu.SMEM)
    body = pl.BlockSpec((ROWS, 128), lambda i: (0, 0))
    whole = lambda *shape: pl.BlockSpec(shape, lambda i: (0,) * len(shape))
    wide = 2 * ORB * PNO
    hi, lo, same = pl.pallas_call(
        gather_kernel,
        grid=(1,),
        in_specs=[meta] * 4 + [body] * 4 + [whole(ORB * PNO, WIDE)],
        out_specs=[whole(ORB * HALF, wide), whole(ORB * HALF, wide), whole(ORB * HALF, WIDE)],
        out_shape=(
            jax.ShapeDtypeStruct((ORB * HALF, wide), BF16),
            jax.ShapeDtypeStruct((ORB * HALF, wide), BF16),
            jax.ShapeDtypeStruct((ORB * HALF, WIDE), F32),
        ),
        scratch_shapes=[pltpu.VMEM((TILES * ORB, HALF, PNO), F32)],
        compiler_params=PARAMS,
        cost_estimate=cost(3 * ORB * HALF * ORB * PNO * WIDE, 4 << 20),
        name="gather",
    )(*halves, *halves, own)

    parts = pl.pallas_call(
        images_kernel,
        out_shape=jax.ShapeDtypeStruct((CHIPS, 2 * HALF, 128), F32),
        compiler_params=PARAMS,
        cost_estimate=cost(3 * ORB * HALF * wide * WIDE, 4 << 20),
        name="images",
    )(hi, lo, same, prev, succ)
    groups = [[2 * z + c for z in range(CHIPS)] for c in range(2)]
    parts = lax.all_to_all(parts, "col", 0, 0, axis_index_groups=groups)

    out = pl.pallas_call(
        density_kernel,
        out_shape=jax.ShapeDtypeStruct((NARROW, AO), F32),
        compiler_params=PARAMS,
        cost_estimate=cost(3 * ORB * PNO * NARROW * AO, 3 << 20),
        name="density",
    )(parts, pno_coef)
    return out.T[None]


def solution(mesh):
    in_specs = (
        P("blk", "col"),
        P("blk", "col"),
        P("blk", "col"),
        P("blk", "col"),
        P("blk", None, None),
        P("blk", "col", None, None),
        P("blk", "col", None, None),
    )
    out_specs = P("blk", None, "col")
    return jax.shard_map(local, mesh=mesh, in_specs=in_specs, out_specs=out_specs, check_vma=False)
```

```python
import jax
import jax.numpy as jnp
from jax import lax
from jax.experimental import pallas as pl
from jax.experimental.pallas import tpu as pltpu
from jax.sharding import PartitionSpec as P

F32 = jnp.float32
BF16 = jnp.bfloat16
ORB = 4
PNO = 128
AO = 1024
SLOTS = 16
CHIPS = 8
WIDE = AO // 2
NARROW = AO // 16
HALF = PNO // 2
ROWS = SLOTS * HALF
META = 8
TILES = 3 * ORB


def split(x):
    hi = x.astype(BF16)
    return hi, (x - hi.astype(F32)).astype(BF16)


def dot(a, b, dims=((1,), (0,))):
    return lax.dot_general(a, b, (dims, ((), ())), preferred_element_type=F32)


def dot3(a, b, dims=((1,), (0,))):
    return dot(a[0], b[0], dims) + (dot(a[0], b[1], dims) + dot(a[1], b[0], dims))


def select_kernel(occ_ref, offset_ref, other_ref, blocks_ref, coef_ref, out_ref, meta_ref, keep_ref, held, numbers, sems):
    copies = [
        pltpu.make_async_copy(coef_ref.at[o, pl.ds(h * HALF, HALF)], held.at[o, pl.ds(h * HALF, HALF)], sems.at[o * 2 + h])
        for o in range(ORB)
        for h in range(2)
    ]
    lists = [
        pltpu.make_async_copy(ref, numbers.at[pl.ds(i, 1)], sems.at[2 * ORB + i])
        for i, ref in enumerate((occ_ref, offset_ref, other_ref, blocks_ref))
    ]
    for copy in lists + copies:
        copy.start()
    for copy in lists:
        copy.wait()
    lane = lax.broadcasted_iota(jnp.int32, (META, 128), 1)
    meta = jnp.zeros((META, 128), jnp.int32)
    for p in range(SLOTS):
        block = (numbers[1, p] * ORB + numbers[2, p]) * ORB + numbers[0, p]
        meta = jnp.where(lane == p, block, meta)
        keep_ref[p] = jnp.full((8, 128), PNO // 4 * numbers[3, p], jnp.int32)
    meta_ref[...] = meta.astype(F32)
    first = lax.axis_index("col") % 2 == 0
    left = lax.broadcasted_iota(jnp.int32, (HALF, 128), 1) < NARROW
    for i, copy in enumerate(copies):
        copy.wait()
        rows = slice(i % 2 * HALF, (i % 2 + 1) * HALF)
        for k in range(CHIPS // 2):
            a = held[i // 2, rows, 256 * k : 256 * k + 128]
            b = held[i // 2, rows, 256 * k + 128 : 256 * k + 256]
            moved = pltpu.roll(jnp.where(first, b, a), NARROW, 1)
            out_ref[i * HALF : (i + 1) * HALF, 128 * k : 128 * k + 128] = jnp.where(
                left, jnp.where(first, a, moved), jnp.where(first, moved, b)
            )


def lagrangian_kernel(meta_ref, kept_ref, amp_ref, int_ref, keep_ref, send_ref):
    upper = (lax.axis_index("col") // 2) % 2 == 1
    far = jnp.maximum(
        lax.broadcasted_iota(jnp.int32, (PNO, PNO), 0), lax.broadcasted_iota(jnp.int32, (PNO, PNO), 1)
    )
    for p in range(SLOTS):
        kept = jnp.where(far < kept_ref[p, 0:1, :], amp_ref[0, p], 0.0)
        lag = dot3(split(kept), split(int_ref[0, p]), ((1,), (1,)))
        low, high = lag[:HALF], lag[HALF:]
        at = slice(p * HALF, (p + 1) * HALF)
        keep_ref[at, :] = jnp.where(upper, high, low)
        send_ref[at, :] = jnp.where(upper, low, high)
    keep_ref[ROWS:, :] = meta_ref[...]
    send_ref[ROWS:, :] = meta_ref[...]


def add_slots(block_ref, meta_ref, lag_ref):
    for p in range(SLOTS):
        number = meta_ref[0, p].astype(jnp.int32)
        block_ref[number] += lag_ref[p * HALF : (p + 1) * HALF, :]


def gather_kernel(m0, m1, m2, l0, l1, l2, block_ref):
    block_ref[...] = jnp.zeros_like(block_ref)
    add_slots(block_ref, m0, l0)
    add_slots(block_ref, m1, l1)
    add_slots(block_ref, m2, l2)


def images_kernel(meta_ref, lag_ref, some_ref, prev_ref, own_ref, next_ref, out_ref, block_ref):
    add_slots(block_ref, meta_ref, lag_ref)
    total = jnp.zeros((ORB * HALF, WIDE), F32)
    for side, x_ref in enumerate((prev_ref, own_ref, next_ref)):
        for j in range(0, ORB, 2):
            lhs = jnp.concatenate(
                [
                    jnp.concatenate([block_ref[(side * ORB + j + i) * ORB + o] for i in range(2)], axis=1)
                    for o in range(ORB)
                ],
                axis=0,
            )
            total += dot3(split(lhs), split(x_ref[j * PNO : (j + 2) * PNO, :]))
    left = lax.broadcasted_iota(jnp.int32, (2 * HALF, 128), 1) < NARROW
    for k in range(CHIPS // 2):
        top = total[: 2 * HALF, 128 * k : 128 * k + 128]
        low = total[2 * HALF :, 128 * k : 128 * k + 128]
        out_ref[2 * k] = jnp.where(left, top, pltpu.roll(low, NARROW, 1))
        out_ref[2 * k + 1] = jnp.where(left, pltpu.roll(top, NARROW, 1), low)


def density_kernel(part_ref, coef_ref, out_ref):
    sums = []
    for h in range(2):
        s = (part_ref[h] + part_ref[h + 2]) + (part_ref[h + 4] + part_ref[h + 6])
        sums.append(s.T)
    total = jnp.zeros((NARROW, AO), F32)
    for pair in range(2):
        lhs = jnp.concatenate([s[NARROW * pair : NARROW * (pair + 1)] for s in sums], axis=1)
        rhs = jnp.concatenate(
            [coef_ref[2 * pair + o, HALF * h : HALF * (h + 1), :] for h in range(2) for o in range(2)],
            axis=0,
        )
        total += dot3(split(lhs), split(rhs))
    out_ref[...] = total


def cost(macs, size):
    return pl.CostEstimate(flops=2 * macs, bytes_accessed=size, transcendentals=0)


PARAMS = pltpu.CompilerParams(vmem_limit_bytes=48 * 1024 * 1024)


def local(pair_occ, pair_offset, pair_other, pno_blocks, pno_coef, amplitudes, integrals):
    tiles = lax.axis_size("blk")
    devices = lax.axis_size("col")
    whole = lambda *shape: pl.BlockSpec(shape, lambda i: (0,) * len(shape))
    in_place = lambda x: pltpu.with_memory_space_constraint(x, pltpu.HBM)

    own, numbers, kept = pl.pallas_call(
        select_kernel,
        in_specs=[pl.BlockSpec(memory_space=pltpu.HBM)] * 5,
        out_shape=(
            jax.ShapeDtypeStruct((ORB * PNO, WIDE), F32),
            jax.ShapeDtypeStruct((META, 128), F32),
            jax.ShapeDtypeStruct((SLOTS, 8, 128), jnp.int32),
        ),
        scratch_shapes=[
            pltpu.VMEM((ORB, PNO, AO), F32),
            pltpu.SMEM((4, SLOTS), jnp.int32),
            pltpu.SemaphoreType.DMA((2 * ORB + 4,)),
        ],
        compiler_params=PARAMS,
        cost_estimate=cost(0, 3 << 20),
        name="select",
    )(*map(in_place, (pair_occ, pair_offset, pair_other, pno_blocks, pno_coef)))
    prev = lax.ppermute(own, "blk", [(i, (i + 1) % tiles) for i in range(tiles)])
    succ = lax.ppermute(own, "blk", [((i + 1) % tiles, i) for i in range(tiles)])

    half = jax.ShapeDtypeStruct((ROWS + META, 128), F32)
    keep, send = pl.pallas_call(
        lagrangian_kernel,
        out_shape=(half, half),
        compiler_params=PARAMS,
        cost_estimate=cost(3 * SLOTS * PNO**3, 3 << 20),
        name="lagrangian",
    )(numbers, kept, amplitudes, integrals)

    swap = lambda x, bit: lax.ppermute(x, "col", [(i, i ^ bit) for i in range(devices)])
    far, near = lax.cond(
        pno_blocks[0, 0] > 0,
        lambda keep, send: (swap(send, 2), swap(keep, 1)),
        lambda keep, send: (jnp.zeros_like(send), jnp.zeros_like(keep)),
        *(keep, send),
    )
    last = swap(far, 1)

    meta = pl.BlockSpec((META, 128), lambda i: (ROWS // META, 0), memory_space=pltpu.SMEM)
    body = pl.BlockSpec((ROWS, 128), lambda i: (0, 0))
    blocks = (TILES * ORB, HALF, PNO)
    some = pl.pallas_call(
        gather_kernel,
        grid=(1,),
        in_specs=[meta] * 3 + [body] * 3,
        out_specs=whole(*blocks),
        out_shape=jax.ShapeDtypeStruct(blocks, F32),
        compiler_params=PARAMS,
        cost_estimate=cost(0, 0),
        name="gather",
    )(keep, near, far, keep, near, far)
    tile = whole(ORB * PNO, WIDE)
    parts, _ = pl.pallas_call(
        images_kernel,
        grid=(1,),
        in_specs=[meta, body, whole(*blocks), tile, tile, tile],
        out_specs=[whole(CHIPS, 2 * HALF, 128), whole(*blocks)],
        out_shape=(
            jax.ShapeDtypeStruct((CHIPS, 2 * HALF, 128), F32),
            jax.ShapeDtypeStruct(blocks, F32),
        ),
        input_output_aliases={2: 1},
        compiler_params=PARAMS,
        cost_estimate=cost(3 * ORB * HALF * TILES * PNO * WIDE, 4 << 20),
        name="images",
    )(last, last, some, prev, own, succ)
    groups = [[2 * z + c for z in range(CHIPS)] for c in range(2)]
    parts = lax.all_to_all(parts, "col", 0, 0, axis_index_groups=groups)

    out = pl.pallas_call(
        density_kernel,
        out_shape=jax.ShapeDtypeStruct((NARROW, AO), F32),
        compiler_params=PARAMS,
        cost_estimate=cost(3 * ORB * PNO * NARROW * AO, 3 << 20),
        name="density",
    )(parts, pno_coef)
    return out.T[None]


def solution(mesh):
    in_specs = (
        P("blk", "col"),
        P("blk", "col"),
        P("blk", "col"),
        P("blk", "col"),
        P("blk", None, None),
        P("blk", "col", None, None),
        P("blk", "col", None, None),
    )
    out_specs = P("blk", None, "col")
    return jax.shard_map(local, mesh=mesh, in_specs=in_specs, out_specs=out_specs, check_vma=False)
```

```python
import functools

import jax
import jax.numpy as jnp
from jax import lax
from jax.experimental import pallas as pl
from jax.experimental.pallas import tpu as pltpu
from jax.sharding import PartitionSpec as P

F32 = jnp.float32
BF16 = jnp.bfloat16
ORB = 4
PNO = 128
AO = 1024
SLOTS = 16
CHIPS = 8
WIDE = AO // 2
NARROW = AO // 16
HALF = PNO // 2
ROWS = SLOTS * HALF
META = 8
TILES = 3 * ORB
ARRIVAL = 1 << 33


def split(x):
    hi = x.astype(BF16)
    return hi, (x - hi.astype(F32)).astype(BF16)


def dot(a, b, dims=((1,), (0,))):
    return lax.dot_general(a, b, (dims, ((), ())), preferred_element_type=F32)


def dot3(a, b, dims=((1,), (0,))):
    return dot(a[0], b[0], dims) + (dot(a[0], b[1], dims) + dot(a[1], b[0], dims))


def select_kernel(occ_ref, offset_ref, other_ref, blocks_ref, coef_ref, out_ref, meta_ref, keep_ref, held, numbers, sems):
    copies = [pltpu.make_async_copy(coef_ref.at[o], held.at[o], sems.at[o]) for o in range(ORB)]
    lists = [
        pltpu.make_async_copy(ref, numbers.at[pl.ds(i, 1)], sems.at[ORB + i])
        for i, ref in enumerate((occ_ref, offset_ref, other_ref, blocks_ref))
    ]
    for copy in copies + lists:
        copy.start()
    for copy in lists:
        copy.wait()
    lane = lax.broadcasted_iota(jnp.int32, (META, 128), 1)
    meta = jnp.zeros((META, 128), jnp.int32)
    for p in range(SLOTS):
        block = (numbers[1, p] * ORB + numbers[2, p]) * ORB + numbers[0, p]
        meta = jnp.where(lane == p, block, meta)
        keep_ref[p] = jnp.full((8, 128), PNO // 4 * numbers[3, p], jnp.int32)
    meta_ref[...] = meta.astype(F32)
    left = lax.broadcasted_iota(jnp.int32, (PNO, 128), 1) < NARROW

    def take(core):
        for o, copy in enumerate(copies):
            copy.wait()
            for k in range(CHIPS // 2):
                a = held[o, :, 256 * k : 256 * k + 128]
                b = held[o, :, 256 * k + 128 : 256 * k + 256]
                a, b = (a, pltpu.roll(b, NARROW, 1)) if core == 0 else (pltpu.roll(a, NARROW, 1), b)
                out_ref[o * PNO : (o + 1) * PNO, 128 * k : 128 * k + 128] = jnp.where(left, a, b)

    for core in range(2):
        pl.when(lax.axis_index("col") % 2 == core)(functools.partial(take, core))


def lagrangian_kernel(meta_ref, kept_ref, amp_ref, int_ref, keep_ref, send_ref):
    upper = (lax.axis_index("col") // 2) % 2 == 1
    far = jnp.maximum(
        lax.broadcasted_iota(jnp.int32, (PNO, PNO), 0), lax.broadcasted_iota(jnp.int32, (PNO, PNO), 1)
    )
    for p in range(SLOTS):
        kept = jnp.where(far < kept_ref[p, 0:1, :], amp_ref[0, p], 0.0)
        lag = dot3(split(kept), split(int_ref[0, p]), ((1,), (1,)))
        low, high = lag[:HALF], lag[HALF:]
        at = slice(p * HALF, (p + 1) * HALF)
        keep_ref[at, :] = jnp.where(upper, high, low)
        send_ref[at, :] = jnp.where(upper, low, high)
    keep_ref[ROWS:, :] = meta_ref[...]
    send_ref[ROWS:, :] = meta_ref[...]


def add_slots(block_ref, lag_ref):
    for p in range(SLOTS):
        number = lag_ref[ROWS, p].astype(jnp.int32)
        block_ref[number] += lag_ref[p * HALF : (p + 1) * HALF, :]


def gather_kernel(keep_ref, near_ref, far_ref, block_ref):
    block_ref[...] = jnp.zeros_like(block_ref)
    for lag_ref in (keep_ref, near_ref, far_ref):
        add_slots(block_ref, lag_ref)


def arrived_kernel(second_ref, first_ref, second_out, first_out):
    pass


def images_kernel(lag_ref, some_ref, second_ref, own_ref, first_ref, out_ref, block_ref):
    add_slots(block_ref, lag_ref)
    odd = lax.axis_index("blk") % 2
    total = jnp.zeros((ORB * HALF, WIDE), F32)
    for start, x_ref in ((ORB, own_ref), (2 * ORB * odd, first_ref), (2 * ORB * (1 - odd), second_ref)):
        lhs = jnp.concatenate(
            [
                jnp.concatenate([block_ref[(start + j) * ORB + o] for j in range(ORB)], axis=1)
                for o in range(ORB)
            ],
            axis=0,
        )
        total += dot3(split(lhs), split(x_ref[...]))
    left = lax.broadcasted_iota(jnp.int32, (2 * HALF, 128), 1) < NARROW
    for k in range(CHIPS // 2):
        top = total[: 2 * HALF, 128 * k : 128 * k + 128]
        low = total[2 * HALF :, 128 * k : 128 * k + 128]
        out_ref[2 * k] = jnp.where(left, top, pltpu.roll(low, NARROW, 1))
        out_ref[2 * k + 1] = jnp.where(left, pltpu.roll(top, NARROW, 1), low)


def density_kernel(part_ref, coef_ref, out_ref, held, sems):
    sums = []
    for h in range(2):
        s = (part_ref[h] + part_ref[h + 2]) + (part_ref[h + 4] + part_ref[h + 6])
        sums.append(s.T)
    lhs = jnp.concatenate([s[NARROW * pair : NARROW * (pair + 1)] for pair in range(2) for s in sums], axis=1)
    lhs = jnp.concatenate(split(lhs))
    copies = []
    for n in range(4):
        at = slice(256 * n, 256 * (n + 1))
        rhs = [
            coef_ref[2 * pair + o, HALF * h : HALF * (h + 1), at]
            for pair in range(2)
            for h in range(2)
            for o in range(2)
        ]
        hi, lo = split(jnp.concatenate(rhs, axis=0))
        both = dot(lhs, hi)
        held[:, at] = both[:NARROW] + (both[NARROW:] + dot(lhs[:NARROW], lo))
        copies.append(pltpu.make_async_copy(held.at[:, at], out_ref.at[:, at], sems.at[n]))
        copies[-1].start()
    for copy in copies:
        copy.wait()


def cost(macs, size):
    return pl.CostEstimate(flops=2 * macs, bytes_accessed=size, transcendentals=0)


PARAMS = pltpu.CompilerParams(vmem_limit_bytes=48 * 1024 * 1024)


def local(pair_occ, pair_offset, pair_other, pno_blocks, pno_coef, amplitudes, integrals):
    tiles = lax.axis_size("blk")
    devices = lax.axis_size("col")
    in_place = lambda x: pltpu.with_memory_space_constraint(x, pltpu.HBM)

    own, numbers, kept = pl.pallas_call(
        select_kernel,
        in_specs=[pl.BlockSpec(memory_space=pltpu.HBM)] * 5,
        out_shape=(
            jax.ShapeDtypeStruct((ORB * PNO, WIDE), F32),
            jax.ShapeDtypeStruct((META, 128), F32),
            jax.ShapeDtypeStruct((SLOTS, 8, 128), jnp.int32),
        ),
        scratch_shapes=[
            pltpu.VMEM((ORB, PNO, AO), F32),
            pltpu.SMEM((4, SLOTS), jnp.int32),
            pltpu.SemaphoreType.DMA((ORB + 4,)),
        ],
        compiler_params=PARAMS,
        cost_estimate=cost(0, 3 << 20),
        name="select",
    )(*map(in_place, (pair_occ, pair_offset, pair_other, pno_blocks, pno_coef)))
    second = lax.ppermute(own, "blk", [(i, (i + 1 - 2 * (i % 2)) % tiles) for i in range(tiles)])
    first = lax.ppermute(own, "blk", [(i, (i + 2 * (i % 2) - 1) % tiles) for i in range(tiles)])

    half = jax.ShapeDtypeStruct((ROWS + META, 128), F32)
    keep, send = pl.pallas_call(
        lagrangian_kernel,
        out_shape=(half, half),
        compiler_params=PARAMS,
        cost_estimate=cost(3 * SLOTS * PNO**3, 3 << 20),
        name="lagrangian",
    )(numbers, kept, amplitudes, integrals)

    swap = lambda x, bit: lax.ppermute(x, "col", [(i, i ^ bit) for i in range(devices)])
    far, near = swap(send, 2), swap(keep, 1)
    last = swap(far, 1)

    blocks = jax.ShapeDtypeStruct((TILES * ORB, HALF, PNO), F32)
    some = pl.pallas_call(
        gather_kernel,
        out_shape=blocks,
        compiler_params=PARAMS,
        cost_estimate=cost(0, 0),
        name="gather",
    )(keep, near, far)
    anywhere = [pl.BlockSpec(memory_space=pl.ANY)] * 2
    second, first = pl.pallas_call(
        arrived_kernel,
        in_specs=anywhere,
        out_specs=anywhere,
        out_shape=(jax.ShapeDtypeStruct(own.shape, F32),) * 2,
        input_output_aliases={0: 0, 1: 1},
        compiler_params=PARAMS,
        cost_estimate=cost(ARRIVAL, 0),
        name="arrived",
    )(second, first)
    parts, _ = pl.pallas_call(
        images_kernel,
        out_shape=(jax.ShapeDtypeStruct((CHIPS, 2 * HALF, 128), F32), blocks),
        input_output_aliases={1: 1},
        compiler_params=PARAMS,
        cost_estimate=cost(3 * ORB * HALF * TILES * PNO * WIDE, 4 << 20),
        name="images",
    )(last, some, second, own, first)
    groups = [[2 * z + c for z in range(CHIPS)] for c in range(2)]
    parts = lax.all_to_all(parts, "col", 0, 0, axis_index_groups=groups)

    out = pl.pallas_call(
        density_kernel,
        out_specs=pl.BlockSpec(memory_space=pl.ANY),
        out_shape=jax.ShapeDtypeStruct((NARROW, AO), F32),
        scratch_shapes=[pltpu.VMEM((NARROW, AO), F32), pltpu.SemaphoreType.DMA((4,))],
        compiler_params=PARAMS,
        cost_estimate=cost(3 * ORB * PNO * NARROW * AO, 3 << 20),
        name="density",
    )(parts, pno_coef)
    return out.T[None]


def solution(mesh):
    in_specs = (
        P("blk", "col"),
        P("blk", "col"),
        P("blk", "col"),
        P("blk", "col"),
        P("blk", None, None),
        P("blk", "col", None, None),
        P("blk", "col", None, None),
    )
    out_specs = P("blk", None, "col")
    return jax.shard_map(local, mesh=mesh, in_specs=in_specs, out_specs=out_specs, check_vma=False)
```

```python
import functools

import jax
import jax.numpy as jnp
from jax import lax
from jax.experimental import pallas as pl
from jax.experimental.pallas import tpu as pltpu
from jax.sharding import PartitionSpec as P

F32 = jnp.float32
BF16 = jnp.bfloat16
ORB = 4
PNO = 128
AO = 1024
SLOTS = 16
CHIPS = 8
WIDE = AO // 2
ORDER = (6, 7, 4, 5, 3, 2, 1, 0)
NARROW = AO // 16
HALF = PNO // 2
ROWS = SLOTS * HALF
META = 8
TILES = 3 * ORB
ARRIVAL = 1 << 33


def split(x):
    hi = x.astype(BF16)
    return hi, (x - hi.astype(F32)).astype(BF16)


def dot(a, b, dims=((1,), (0,))):
    return lax.dot_general(a, b, (dims, ((), ())), preferred_element_type=F32)


def dot3(a, b, dims=((1,), (0,))):
    return dot(a[0], b[0], dims) + (dot(a[0], b[1], dims) + dot(a[1], b[0], dims))


def select_kernel(occ_ref, offset_ref, other_ref, blocks_ref, coef_ref, out_ref, meta_ref, keep_ref, held, numbers, sems):
    copies = [pltpu.make_async_copy(coef_ref.at[o], held.at[o], sems.at[o]) for o in range(ORB)]
    lists = [
        pltpu.make_async_copy(ref, numbers.at[pl.ds(i, 1)], sems.at[ORB + i])
        for i, ref in enumerate((occ_ref, offset_ref, other_ref, blocks_ref))
    ]
    for copy in copies + lists:
        copy.start()
    for copy in lists:
        copy.wait()
    lane = lax.broadcasted_iota(jnp.int32, (META, 128), 1)
    meta = jnp.zeros((META, 128), jnp.int32)
    for p in range(SLOTS):
        block = (numbers[1, p] * ORB + numbers[2, p]) * ORB + numbers[0, p]
        meta = jnp.where(lane == p, block, meta)
        keep_ref[p] = jnp.full((8, 128), PNO // 4 * numbers[3, p], jnp.int32)
    meta_ref[...] = meta.astype(F32)
    left = lax.broadcasted_iota(jnp.int32, (PNO, 128), 1) < NARROW

    def take(core):
        for o, copy in enumerate(copies):
            copy.wait()
            for k in range(CHIPS // 2):
                a = held[o, :, 256 * k : 256 * k + 128]
                b = held[o, :, 256 * k + 128 : 256 * k + 256]
                a, b = (a, pltpu.roll(b, NARROW, 1)) if core == 0 else (pltpu.roll(a, NARROW, 1), b)
                out_ref[o * PNO : (o + 1) * PNO, 128 * k : 128 * k + 128] = jnp.where(left, a, b)

    for core in range(2):
        pl.when(lax.axis_index("col") % 2 == core)(functools.partial(take, core))


def lagrangian_kernel(meta_ref, kept_ref, amp_ref, int_ref, keep_ref, send_ref):
    upper = (lax.axis_index("col") // 2) % 2 == 1
    far = jnp.maximum(
        lax.broadcasted_iota(jnp.int32, (PNO, PNO), 0), lax.broadcasted_iota(jnp.int32, (PNO, PNO), 1)
    )
    for p in range(SLOTS):
        kept = jnp.where(far < kept_ref[p, 0:1, :], amp_ref[0, p], 0.0)
        lag = dot3(split(kept), split(int_ref[0, p]), ((1,), (1,)))
        low, high = lag[:HALF], lag[HALF:]
        at = slice(p * HALF, (p + 1) * HALF)
        keep_ref[at, :] = jnp.where(upper, high, low)
        send_ref[at, :] = jnp.where(upper, low, high)
    keep_ref[ROWS:, :] = meta_ref[...]
    send_ref[ROWS:, :] = meta_ref[...]


def add_slots(block_ref, lag_ref):
    for p in range(SLOTS):
        number = lag_ref[ROWS, p].astype(jnp.int32)
        block_ref[number] += lag_ref[p * HALF : (p + 1) * HALF, :]


def gather_kernel(keep_ref, near_ref, far_ref, block_ref):
    block_ref[...] = jnp.zeros_like(block_ref)
    for lag_ref in (keep_ref, near_ref, far_ref):
        add_slots(block_ref, lag_ref)


def arrived_kernel(second_ref, first_ref, second_out, first_out):
    pass


def images_kernel(lag_ref, some_ref, second_ref, own_ref, first_ref, out_ref, block_ref):
    add_slots(block_ref, lag_ref)
    odd = lax.axis_index("blk") % 2
    total = jnp.zeros((ORB * HALF, WIDE), F32)
    for start, x_ref in ((ORB, own_ref), (2 * ORB * odd, first_ref), (2 * ORB * (1 - odd), second_ref)):
        lhs = jnp.concatenate(
            [
                jnp.concatenate([block_ref[(start + j) * ORB + o] for j in range(ORB)], axis=1)
                for o in range(ORB)
            ],
            axis=0,
        )
        total += dot3(split(lhs), split(x_ref[...]))
    left = lax.broadcasted_iota(jnp.int32, (2 * HALF, 128), 1) < NARROW
    for k in range(CHIPS // 2):
        top = total[: 2 * HALF, 128 * k : 128 * k + 128]
        low = total[2 * HALF :, 128 * k : 128 * k + 128]
        out_ref[ORDER.index(2 * k)] = jnp.where(left, top, pltpu.roll(low, NARROW, 1))
        out_ref[ORDER.index(2 * k + 1)] = jnp.where(left, pltpu.roll(top, NARROW, 1), low)


def density_kernel(part_ref, coef_ref, out_ref, held, sems):
    sums = []
    for h in range(2):
        a, b, c, d = (part_ref[ORDER.index(z)] for z in range(h, CHIPS, 2))
        sums.append(((a + b) + (c + d)).T)
    lhs = jnp.concatenate([s[NARROW * pair : NARROW * (pair + 1)] for pair in range(2) for s in sums], axis=1)
    lhs = jnp.concatenate(split(lhs))
    copies = []
    for n in range(4):
        at = slice(256 * n, 256 * (n + 1))
        rhs = [
            coef_ref[2 * pair + o, HALF * h : HALF * (h + 1), at]
            for pair in range(2)
            for h in range(2)
            for o in range(2)
        ]
        hi, lo = split(jnp.concatenate(rhs, axis=0))
        both = dot(lhs, hi)
        held[:, at] = both[:NARROW] + (both[NARROW:] + dot(lhs[:NARROW], lo))
        copies.append(pltpu.make_async_copy(held.at[:, at], out_ref.at[:, at], sems.at[n]))
        copies[-1].start()
    for copy in copies:
        copy.wait()


def cost(macs, size):
    return pl.CostEstimate(flops=2 * macs, bytes_accessed=size, transcendentals=0)


PARAMS = pltpu.CompilerParams(vmem_limit_bytes=48 * 1024 * 1024)


def local(pair_occ, pair_offset, pair_other, pno_blocks, pno_coef, amplitudes, integrals):
    tiles = lax.axis_size("blk")
    devices = lax.axis_size("col")
    in_place = lambda x: pltpu.with_memory_space_constraint(x, pltpu.HBM)

    own, numbers, kept = pl.pallas_call(
        select_kernel,
        in_specs=[pl.BlockSpec(memory_space=pltpu.HBM)] * 5,
        out_shape=(
            jax.ShapeDtypeStruct((ORB * PNO, WIDE), F32),
            jax.ShapeDtypeStruct((META, 128), F32),
            jax.ShapeDtypeStruct((SLOTS, 8, 128), jnp.int32),
        ),
        scratch_shapes=[
            pltpu.VMEM((ORB, PNO, AO), F32),
            pltpu.SMEM((4, SLOTS), jnp.int32),
            pltpu.SemaphoreType.DMA((ORB + 4,)),
        ],
        compiler_params=PARAMS,
        cost_estimate=cost(0, 3 << 20),
        name="select",
    )(*map(in_place, (pair_occ, pair_offset, pair_other, pno_blocks, pno_coef)))
    second = lax.ppermute(own, "blk", [(i, (i + 1 - 2 * (i % 2)) % tiles) for i in range(tiles)])
    first = lax.ppermute(own, "blk", [(i, (i + 2 * (i % 2) - 1) % tiles) for i in range(tiles)])

    half = jax.ShapeDtypeStruct((ROWS + META, 128), F32)
    keep, send = pl.pallas_call(
        lagrangian_kernel,
        out_shape=(half, half),
        compiler_params=PARAMS,
        cost_estimate=cost(3 * SLOTS * PNO**3, 3 << 20),
        name="lagrangian",
    )(numbers, kept, amplitudes, integrals)

    swap = lambda x, bit: lax.ppermute(x, "col", [(i, i ^ bit) for i in range(devices)])
    far, near = swap(send, 2), swap(keep, 1)
    last = swap(far, 1)

    blocks = jax.ShapeDtypeStruct((TILES * ORB, HALF, PNO), F32)
    some = pl.pallas_call(
        gather_kernel,
        out_shape=blocks,
        compiler_params=PARAMS,
        cost_estimate=cost(0, 0),
        name="gather",
    )(keep, near, far)
    anywhere = [pl.BlockSpec(memory_space=pl.ANY)] * 2
    second, first = pl.pallas_call(
        arrived_kernel,
        in_specs=anywhere,
        out_specs=anywhere,
        out_shape=(jax.ShapeDtypeStruct(own.shape, F32),) * 2,
        input_output_aliases={0: 0, 1: 1},
        compiler_params=PARAMS,
        cost_estimate=cost(ARRIVAL, 0),
        name="arrived",
    )(second, first)
    parts, _ = pl.pallas_call(
        images_kernel,
        out_shape=(jax.ShapeDtypeStruct((CHIPS, 2 * HALF, 128), F32), blocks),
        input_output_aliases={1: 1},
        compiler_params=PARAMS,
        cost_estimate=cost(3 * ORB * HALF * TILES * PNO * WIDE, 4 << 20),
        name="images",
    )(last, some, second, own, first)
    groups = [[2 * z + c for z in ORDER] for c in range(2)]
    parts = lax.all_to_all(parts, "col", 0, 0, axis_index_groups=groups)

    out = pl.pallas_call(
        density_kernel,
        out_specs=pl.BlockSpec(memory_space=pl.ANY),
        out_shape=jax.ShapeDtypeStruct((NARROW, AO), F32),
        scratch_shapes=[pltpu.VMEM((NARROW, AO), F32), pltpu.SemaphoreType.DMA((4,))],
        compiler_params=PARAMS,
        cost_estimate=cost(3 * ORB * PNO * NARROW * AO, 3 << 20),
        name="density",
    )(parts, pno_coef)
    return out.T[None]


def solution(mesh):
    in_specs = (
        P("blk", "col"),
        P("blk", "col"),
        P("blk", "col"),
        P("blk", "col"),
        P("blk", None, None),
        P("blk", "col", None, None),
        P("blk", "col", None, None),
    )
    out_specs = P("blk", None, "col")
    return jax.shard_map(local, mesh=mesh, in_specs=in_specs, out_specs=out_specs, check_vma=False)
```

```python
import functools

import jax
import jax.numpy as jnp
from jax import lax
from jax.experimental import pallas as pl
from jax.experimental.pallas import tpu as pltpu
from jax.sharding import PartitionSpec as P

F32 = jnp.float32
BF16 = jnp.bfloat16
ORB = 4
PNO = 128
AO = 1024
SLOTS = 16
CHIPS = 8
WIDE = AO // 2
ORDER = (6, 7, 4, 5, 3, 2, 1, 0)
NARROW = AO // 16
PART = 16
HELD = 3 * PART
FEWER = 2 * PART
META = 8
TILES = 3 * ORB
ARRIVAL = 1 << 33


def split(x):
    hi = x.astype(BF16)
    return hi, (x - hi.astype(F32)).astype(BF16)


def dot(a, b, dims=((1,), (0,))):
    return lax.dot_general(a, b, (dims, ((), ())), preferred_element_type=F32)


def dot3(a, b, dims=((1,), (0,))):
    return dot(a[0], b[0], dims) + (dot(a[0], b[1], dims) + dot(a[1], b[0], dims))


def select_kernel(occ_ref, offset_ref, other_ref, blocks_ref, coef_ref, out_ref, meta_ref, keep_ref, held, numbers, sems):
    copies = [pltpu.make_async_copy(coef_ref.at[o], held.at[o], sems.at[o]) for o in range(ORB)]
    lists = [
        pltpu.make_async_copy(ref, numbers.at[pl.ds(i, 1)], sems.at[ORB + i])
        for i, ref in enumerate((occ_ref, offset_ref, other_ref, blocks_ref))
    ]
    for copy in copies + lists:
        copy.start()
    for copy in lists:
        copy.wait()
    lane = lax.broadcasted_iota(jnp.int32, (META, 128), 1)
    meta = jnp.zeros((META, 128), jnp.int32)
    for p in range(SLOTS):
        block = (numbers[1, p] * ORB + numbers[2, p]) * ORB + numbers[0, p]
        meta = jnp.where(lane == p, block, meta)
        keep_ref[p] = jnp.full((8, 128), PNO // 4 * numbers[3, p], jnp.int32)
    meta_ref[...] = meta.astype(F32)
    left = lax.broadcasted_iota(jnp.int32, (PNO, 128), 1) < NARROW

    def take(core):
        for o, copy in enumerate(copies):
            copy.wait()
            for k in range(CHIPS // 2):
                a = held[o, :, 256 * k : 256 * k + 128]
                b = held[o, :, 256 * k + 128 : 256 * k + 256]
                a, b = (a, pltpu.roll(b, NARROW, 1)) if core == 0 else (pltpu.roll(a, NARROW, 1), b)
                out_ref[o * PNO : (o + 1) * PNO, 128 * k : 128 * k + 128] = jnp.where(left, a, b)

    for core in range(2):
        pl.when(lax.axis_index("col") % 2 == core)(functools.partial(take, core))


def lagrangian_kernel(meta_ref, kept_ref, amp_ref, int_ref, keep_ref, up_ref, down_ref, held):
    far = jnp.maximum(
        lax.broadcasted_iota(jnp.int32, (PNO, PNO), 0), lax.broadcasted_iota(jnp.int32, (PNO, PNO), 1)
    )
    for p in range(SLOTS):
        kept = jnp.where(far < kept_ref[p, 0:1, :], amp_ref[0, p], 0.0)
        held[p] = dot3(split(kept), split(int_ref[0, p]), ((1,), (1,)))
    chip = lax.axis_index("col") // 2
    for ref, step, size in ((keep_ref, 0, HELD), (up_ref, 1, HELD), (down_ref, -1, FEWER)):
        for t in range(size // PART):
            start = pl.multiple_of((chip + step - 3 * t + CHIPS) % CHIPS * PART, PART)
            for p in range(SLOTS):
                at = p * size + t * PART
                ref[at : at + PART, :] = held[p, pl.ds(start, PART), :]
        ref[SLOTS * size :, :] = meta_ref[...]


def gather_kernel(keep_ref, below_ref, above_ref, block_ref):
    block_ref[...] = jnp.zeros_like(block_ref)
    for lag_ref, size in ((keep_ref, HELD), (below_ref, HELD), (above_ref, FEWER)):
        for p in range(SLOTS):
            number = lag_ref[SLOTS * size, p].astype(jnp.int32)
            block_ref[number, :size, :] += lag_ref[p * size : (p + 1) * size, :]


def arrived_kernel(second_ref, first_ref, second_out, first_out):
    pass


def images_kernel(mine_ref, other_ref, second_ref, own_ref, first_ref, out_ref):
    odd = (lax.axis_index("blk") + lax.axis_index("col")) % 2
    size = ORB * HELD
    total = jnp.zeros((size, WIDE), F32)
    for start, x_ref in ((ORB, own_ref), (2 * ORB * odd, first_ref), (2 * ORB * (1 - odd), second_ref)):
        lhs = jnp.concatenate(
            [
                jnp.concatenate(
                    [mine_ref[(start + j) * ORB + o] + other_ref[(start + j) * ORB + o] for j in range(ORB)], axis=1
                )
                for o in range(ORB)
            ],
            axis=0,
        )
        hi, lo = split(lhs)
        x_hi, x_lo = split(x_ref[...])
        both = dot(jnp.concatenate([hi, lo]), x_hi)
        total += both[:size] + (both[size:] + dot(hi, x_lo))
    left = lax.broadcasted_iota(jnp.int32, (size // 2, 128), 1) < NARROW
    for k in range(CHIPS // 2):
        top = total[: size // 2, 128 * k : 128 * k + 128]
        low = total[size // 2 :, 128 * k : 128 * k + 128]
        out_ref[ORDER.index(2 * k)] = jnp.where(left, top, pltpu.roll(low, NARROW, 1))
        out_ref[ORDER.index(2 * k + 1)] = jnp.where(left, pltpu.roll(top, NARROW, 1), low)


def density_kernel(part_ref, coef_ref, out_ref, held, sems):
    sums = []
    for r in range(CHIPS):
        for o in range(2):
            a, b, c = (
                part_ref[ORDER.index((r + 3 * t) % CHIPS), o * HELD + t * PART : o * HELD + (t + 1) * PART, :]
                for t in range(3)
            )
            sums.append(a + b + c)
    sums = jnp.concatenate(sums, axis=0).T
    lhs = jnp.concatenate(split(jnp.concatenate([sums[:NARROW], sums[NARROW:]], axis=1)))
    copies = []
    for n in range(4):
        at = slice(256 * n, 256 * (n + 1))
        rhs = [
            coef_ref[2 * pair + o, r * PART : (r + 1) * PART, at]
            for pair in range(2)
            for r in range(CHIPS)
            for o in range(2)
        ]
        hi, lo = split(jnp.concatenate(rhs, axis=0))
        both = dot(lhs, hi)
        held[:, at] = both[:NARROW] + (both[NARROW:] + dot(lhs[:NARROW], lo))
        copies.append(pltpu.make_async_copy(held.at[:, at], out_ref.at[:, at], sems.at[n]))
        copies[-1].start()
    for copy in copies:
        copy.wait()


def cost(macs, size):
    return pl.CostEstimate(flops=2 * macs, bytes_accessed=size, transcendentals=0)


PARAMS = pltpu.CompilerParams(vmem_limit_bytes=48 * 1024 * 1024)


def local(pair_occ, pair_offset, pair_other, pno_blocks, pno_coef, amplitudes, integrals):
    tiles = lax.axis_size("blk")
    devices = lax.axis_size("col")
    in_place = lambda x: pltpu.with_memory_space_constraint(x, pltpu.HBM)

    own, numbers, kept = pl.pallas_call(
        select_kernel,
        in_specs=[pl.BlockSpec(memory_space=pltpu.HBM)] * 5,
        out_shape=(
            jax.ShapeDtypeStruct((ORB * PNO, WIDE), F32),
            jax.ShapeDtypeStruct((META, 128), F32),
            jax.ShapeDtypeStruct((SLOTS, 8, 128), jnp.int32),
        ),
        scratch_shapes=[
            pltpu.VMEM((ORB, PNO, AO), F32),
            pltpu.SMEM((4, SLOTS), jnp.int32),
            pltpu.SemaphoreType.DMA((ORB + 4,)),
        ],
        compiler_params=PARAMS,
        cost_estimate=cost(0, 3 << 20),
        name="select",
    )(*map(in_place, (pair_occ, pair_offset, pair_other, pno_blocks, pno_coef)))
    def halo(turn):
        pairs = []
        for b in range(tiles):
            for q in range(devices):
                there = (b + 2 * ((b + q + turn) % 2) - 1) % tiles
                pairs.append((b * devices + q, there * devices + q))
        return lax.ppermute(own, ("blk", "col"), pairs)

    second, first = halo(1), halo(0)

    pieces = lambda size: jax.ShapeDtypeStruct((SLOTS * size + META, 128), F32)
    keep, up, down = pl.pallas_call(
        lagrangian_kernel,
        out_shape=(pieces(HELD), pieces(HELD), pieces(FEWER)),
        scratch_shapes=[pltpu.VMEM((SLOTS, PNO, PNO), F32)],
        compiler_params=PARAMS,
        cost_estimate=cost(3 * SLOTS * PNO**3, 3 << 20),
        name="lagrangian",
    )(numbers, kept, amplitudes, integrals)

    shift = lambda x, chips: lax.ppermute(x, "col", [(i, (i + 2 * chips) % devices) for i in range(devices)])
    mine = pl.pallas_call(
        gather_kernel,
        out_shape=jax.ShapeDtypeStruct((TILES * ORB, HELD, PNO), F32),
        compiler_params=PARAMS,
        cost_estimate=cost(0, 0),
        name="gather",
    )(keep, shift(up, 1), shift(down, -1))
    other = lax.ppermute(mine, "col", [(i, i ^ 1) for i in range(devices)])

    anywhere = [pl.BlockSpec(memory_space=pl.ANY)] * 2
    second, first = pl.pallas_call(
        arrived_kernel,
        in_specs=anywhere,
        out_specs=anywhere,
        out_shape=(jax.ShapeDtypeStruct(own.shape, F32),) * 2,
        input_output_aliases={0: 0, 1: 1},
        compiler_params=PARAMS,
        cost_estimate=cost(ARRIVAL, 0),
        name="arrived",
    )(second, first)
    parts = pl.pallas_call(
        images_kernel,
        out_shape=jax.ShapeDtypeStruct((CHIPS, ORB * HELD // 2, 128), F32),
        compiler_params=PARAMS,
        cost_estimate=cost(3 * ORB * HELD * TILES * PNO * WIDE, 4 << 20),
        name="images",
    )(mine, other, second, own, first)
    groups = [[2 * z + c for z in ORDER] for c in range(2)]
    parts = lax.all_to_all(parts, "col", 0, 0, axis_index_groups=groups)

    out = pl.pallas_call(
        density_kernel,
        out_specs=pl.BlockSpec(memory_space=pl.ANY),
        out_shape=jax.ShapeDtypeStruct((NARROW, AO), F32),
        scratch_shapes=[pltpu.VMEM((NARROW, AO), F32), pltpu.SemaphoreType.DMA((4,))],
        compiler_params=PARAMS,
        cost_estimate=cost(3 * ORB * PNO * NARROW * AO, 3 << 20),
        name="density",
    )(parts, pno_coef)
    return out.T[None]


def solution(mesh):
    in_specs = (
        P("blk", "col"),
        P("blk", "col"),
        P("blk", "col"),
        P("blk", "col"),
        P("blk", None, None),
        P("blk", "col", None, None),
        P("blk", "col", None, None),
    )
    out_specs = P("blk", None, "col")
    return jax.shard_map(local, mesh=mesh, in_specs=in_specs, out_specs=out_specs, check_vma=False)
```

```python
import functools

import jax
import jax.numpy as jnp
from jax import lax
from jax.experimental import pallas as pl
from jax.experimental.pallas import tpu as pltpu
from jax.sharding import PartitionSpec as P

F32 = jnp.float32
BF16 = jnp.bfloat16
ORB = 4
PNO = 128
AO = 1024
SLOTS = 16
CHIPS = 8
WIDE = AO // 2
ORDER = (6, 7, 4, 5, 3, 2, 1, 0)
NARROW = AO // 16
PART = 16
HELD = 3 * PART
FEWER = 2 * PART
META = 8
TILES = 3 * ORB
ARRIVAL = 1 << 33


def split(x):
    hi = x.astype(BF16)
    return hi, (x - hi.astype(F32)).astype(BF16)


def dot(a, b, dims=((1,), (0,))):
    return lax.dot_general(a, b, (dims, ((), ())), preferred_element_type=F32)


def dot3(a, b, dims=((1,), (0,))):
    return dot(a[0], b[0], dims) + (dot(a[0], b[1], dims) + dot(a[1], b[0], dims))


def select_kernel(occ_ref, offset_ref, other_ref, blocks_ref, coef_ref, out_ref, meta_ref, keep_ref, held, numbers, sems):
    copies = [pltpu.make_async_copy(coef_ref.at[o], held.at[o], sems.at[o]) for o in range(ORB)]
    lists = [
        pltpu.make_async_copy(ref, numbers.at[pl.ds(i, 1)], sems.at[ORB + i])
        for i, ref in enumerate((occ_ref, offset_ref, other_ref, blocks_ref))
    ]
    for copy in copies + lists:
        copy.start()
    for copy in lists:
        copy.wait()
    lane = lax.broadcasted_iota(jnp.int32, (META, 128), 1)
    meta = jnp.zeros((META, 128), jnp.int32)
    for p in range(SLOTS):
        block = (numbers[1, p] * ORB + numbers[2, p]) * ORB + numbers[0, p]
        meta = jnp.where(lane == p, block, meta)
        keep_ref[p] = jnp.full((8, 128), PNO // 4 * numbers[3, p], jnp.int32)
    meta_ref[...] = meta.astype(F32)
    left = lax.broadcasted_iota(jnp.int32, (PNO, 128), 1) < NARROW

    def take(core):
        for o, copy in enumerate(copies):
            copy.wait()
            for k in range(CHIPS // 2):
                a = held[o, :, 256 * k : 256 * k + 128]
                b = held[o, :, 256 * k + 128 : 256 * k + 256]
                a, b = (a, pltpu.roll(b, NARROW, 1)) if core == 0 else (pltpu.roll(a, NARROW, 1), b)
                out_ref[o * PNO : (o + 1) * PNO, 128 * k : 128 * k + 128] = jnp.where(left, a, b)

    for core in range(2):
        pl.when(lax.axis_index("col") % 2 == core)(functools.partial(take, core))


def lagrangian_kernel(meta_ref, kept_ref, amp_ref, int_ref, keep_ref, up_ref, down_ref, held):
    far = jnp.maximum(
        lax.broadcasted_iota(jnp.int32, (PNO, PNO), 0), lax.broadcasted_iota(jnp.int32, (PNO, PNO), 1)
    )
    for p in range(SLOTS):
        kept = jnp.where(far < kept_ref[p, 0:1, :], amp_ref[0, p], 0.0)
        held[p] = dot3(split(kept), split(int_ref[0, p]), ((1,), (1,)))
    chip = lax.axis_index("col") // 2
    for ref, step, size in ((keep_ref, 0, HELD), (up_ref, 1, HELD), (down_ref, -1, FEWER)):
        for t in range(size // PART):
            start = pl.multiple_of((chip + step - 3 * t + CHIPS) % CHIPS * PART, PART)
            for p in range(SLOTS):
                at = p * size + t * PART
                ref[at : at + PART, :] = held[p, pl.ds(start, PART), :]
        ref[SLOTS * size :, :] = meta_ref[...]


def gather_kernel(keep_ref, below_ref, above_ref, block_ref):
    block_ref[...] = jnp.zeros_like(block_ref)
    for lag_ref, size in ((keep_ref, HELD), (below_ref, HELD), (above_ref, FEWER)):
        for p in range(SLOTS):
            number = lag_ref[SLOTS * size, p].astype(jnp.int32)
            block_ref[number, :size, :] += lag_ref[p * size : (p + 1) * size, :]


def arrived_kernel(second_ref, first_ref, second_out, first_out):
    pass


def images_kernel(mine_ref, other_ref, second_ref, own_ref, first_ref, out_ref):
    odd = (lax.axis_index("blk") + lax.axis_index("col") + 1) % 2
    size = ORB * HELD
    total = jnp.zeros((size, WIDE), F32)
    for start, x_ref in ((ORB, own_ref), (2 * ORB * odd, first_ref), (2 * ORB * (1 - odd), second_ref)):
        lhs = jnp.concatenate(
            [
                jnp.concatenate(
                    [mine_ref[(start + j) * ORB + o] + other_ref[(start + j) * ORB + o] for j in range(ORB)], axis=1
                )
                for o in range(ORB)
            ],
            axis=0,
        )
        hi, lo = split(lhs)
        x_hi, x_lo = split(x_ref[...])
        both = dot(jnp.concatenate([hi, lo]), x_hi)
        total += both[:size] + (both[size:] + dot(hi, x_lo))
    left = lax.broadcasted_iota(jnp.int32, (size // 2, 128), 1) < NARROW
    for k in range(CHIPS // 2):
        top = total[: size // 2, 128 * k : 128 * k + 128]
        low = total[size // 2 :, 128 * k : 128 * k + 128]
        out_ref[ORDER.index(2 * k)] = jnp.where(left, top, pltpu.roll(low, NARROW, 1))
        out_ref[ORDER.index(2 * k + 1)] = jnp.where(left, pltpu.roll(top, NARROW, 1), low)


def density_kernel(part_ref, coef_ref, out_ref, held, sems):
    sums = []
    for r in range(CHIPS):
        for o in range(2):
            a, b, c = (
                part_ref[ORDER.index((r + 3 * t) % CHIPS), o * HELD + t * PART : o * HELD + (t + 1) * PART, :]
                for t in range(3)
            )
            sums.append(a + b + c)
    sums = jnp.concatenate(sums, axis=0).T
    lhs = jnp.concatenate(split(jnp.concatenate([sums[:NARROW], sums[NARROW:]], axis=1)))
    copies = []
    for n in range(4):
        at = slice(256 * n, 256 * (n + 1))
        rhs = [
            coef_ref[2 * pair + o, r * PART : (r + 1) * PART, at]
            for pair in range(2)
            for r in range(CHIPS)
            for o in range(2)
        ]
        hi, lo = split(jnp.concatenate(rhs, axis=0))
        both = dot(lhs, hi)
        held[:, at] = both[:NARROW] + (both[NARROW:] + dot(lhs[:NARROW], lo))
        copies.append(pltpu.make_async_copy(held.at[:, at], out_ref.at[:, at], sems.at[n]))
        copies[-1].start()
    for copy in copies:
        copy.wait()


def cost(macs, size):
    return pl.CostEstimate(flops=2 * macs, bytes_accessed=size, transcendentals=0)


PARAMS = pltpu.CompilerParams(vmem_limit_bytes=48 * 1024 * 1024)


def local(pair_occ, pair_offset, pair_other, pno_blocks, pno_coef, amplitudes, integrals):
    tiles = lax.axis_size("blk")
    devices = lax.axis_size("col")
    in_place = lambda x: pltpu.with_memory_space_constraint(x, pltpu.HBM)

    own, numbers, kept = pl.pallas_call(
        select_kernel,
        in_specs=[pl.BlockSpec(memory_space=pltpu.HBM)] * 5,
        out_shape=(
            jax.ShapeDtypeStruct((ORB * PNO, WIDE), F32),
            jax.ShapeDtypeStruct((META, 128), F32),
            jax.ShapeDtypeStruct((SLOTS, 8, 128), jnp.int32),
        ),
        scratch_shapes=[
            pltpu.VMEM((ORB, PNO, AO), F32),
            pltpu.SMEM((4, SLOTS), jnp.int32),
            pltpu.SemaphoreType.DMA((ORB + 4,)),
        ],
        compiler_params=PARAMS,
        cost_estimate=cost(0, 3 << 20),
        name="select",
    )(*map(in_place, (pair_occ, pair_offset, pair_other, pno_blocks, pno_coef)))
    def halo(turn):
        pairs = []
        for b in range(tiles):
            for q in range(devices):
                there = (b + 2 * ((b + q + turn) % 2) - 1) % tiles
                pairs.append((b * devices + q, there * devices + q))
        return lax.ppermute(own, ("blk", "col"), pairs)

    second, first = halo(0), halo(1)

    pieces = lambda size: jax.ShapeDtypeStruct((SLOTS * size + META, 128), F32)
    keep, up, down = pl.pallas_call(
        lagrangian_kernel,
        out_shape=(pieces(HELD), pieces(HELD), pieces(FEWER)),
        scratch_shapes=[pltpu.VMEM((SLOTS, PNO, PNO), F32)],
        compiler_params=PARAMS,
        cost_estimate=cost(3 * SLOTS * PNO**3, 3 << 20),
        name="lagrangian",
    )(numbers, kept, amplitudes, integrals)

    shift = lambda x, chips: lax.ppermute(x, "col", [(i, (i + 2 * chips) % devices) for i in range(devices)])
    mine = pl.pallas_call(
        gather_kernel,
        out_shape=jax.ShapeDtypeStruct((TILES * ORB, HELD, PNO), F32),
        compiler_params=PARAMS,
        cost_estimate=cost(0, 0),
        name="gather",
    )(keep, shift(up, 1), shift(down, -1))
    other = lax.ppermute(mine, "col", [(i, i ^ 1) for i in range(devices)])

    anywhere = [pl.BlockSpec(memory_space=pl.ANY)] * 2
    second, first = pl.pallas_call(
        arrived_kernel,
        in_specs=anywhere,
        out_specs=anywhere,
        out_shape=(jax.ShapeDtypeStruct(own.shape, F32),) * 2,
        input_output_aliases={0: 0, 1: 1},
        compiler_params=PARAMS,
        cost_estimate=cost(ARRIVAL, 0),
        name="arrived",
    )(second, first)
    parts = pl.pallas_call(
        images_kernel,
        out_shape=jax.ShapeDtypeStruct((CHIPS, ORB * HELD // 2, 128), F32),
        compiler_params=PARAMS,
        cost_estimate=cost(3 * ORB * HELD * TILES * PNO * WIDE, 4 << 20),
        name="images",
    )(mine, other, second, own, first)
    groups = [[2 * z + c for z in ORDER] for c in range(2)]
    parts = lax.all_to_all(parts, "col", 0, 0, axis_index_groups=groups)

    out = pl.pallas_call(
        density_kernel,
        out_specs=pl.BlockSpec(memory_space=pl.ANY),
        out_shape=jax.ShapeDtypeStruct((NARROW, AO), F32),
        scratch_shapes=[pltpu.VMEM((NARROW, AO), F32), pltpu.SemaphoreType.DMA((4,))],
        compiler_params=PARAMS,
        cost_estimate=cost(3 * ORB * PNO * NARROW * AO, 3 << 20),
        name="density",
    )(parts, pno_coef)
    return out.T[None]


def solution(mesh):
    in_specs = (
        P("blk", "col"),
        P("blk", "col"),
        P("blk", "col"),
        P("blk", "col"),
        P("blk", None, None),
        P("blk", "col", None, None),
        P("blk", "col", None, None),
    )
    out_specs = P("blk", None, "col")
    return jax.shard_map(local, mesh=mesh, in_specs=in_specs, out_specs=out_specs, check_vma=False)
```

```python
import functools

import jax
import jax.numpy as jnp
from jax import lax
from jax.experimental import pallas as pl
from jax.experimental.pallas import tpu as pltpu
from jax.sharding import PartitionSpec as P

F32 = jnp.float32
BF16 = jnp.bfloat16
ORB = 4
PNO = 128
AO = 1024
SLOTS = 16
CHIPS = 8
WIDE = AO // 2
ORDER = (7, 4, 6, 5, 3, 2, 1, 0)
NARROW = AO // 16
PART = 16
HELD = 3 * PART
FEWER = 2 * PART
META = 8
TILES = 3 * ORB
ARRIVAL = 1 << 33


def split(x):
    hi = x.astype(BF16)
    return hi, (x - hi.astype(F32)).astype(BF16)


def dot(a, b, dims=((1,), (0,))):
    return lax.dot_general(a, b, (dims, ((), ())), preferred_element_type=F32)


def dot3(a, b, dims=((1,), (0,))):
    return dot(a[0], b[0], dims) + (dot(a[0], b[1], dims) + dot(a[1], b[0], dims))


def select_kernel(occ_ref, offset_ref, other_ref, blocks_ref, coef_ref, out_ref, meta_ref, keep_ref, held, numbers, sems):
    copies = [pltpu.make_async_copy(coef_ref.at[o], held.at[o], sems.at[o]) for o in range(ORB)]
    lists = [
        pltpu.make_async_copy(ref, numbers.at[pl.ds(i, 1)], sems.at[ORB + i])
        for i, ref in enumerate((occ_ref, offset_ref, other_ref, blocks_ref))
    ]
    for copy in copies + lists:
        copy.start()
    for copy in lists:
        copy.wait()
    lane = lax.broadcasted_iota(jnp.int32, (META, 128), 1)
    meta = jnp.zeros((META, 128), jnp.int32)
    for p in range(SLOTS):
        block = (numbers[1, p] * ORB + numbers[2, p]) * ORB + numbers[0, p]
        meta = jnp.where(lane == p, block, meta)
        keep_ref[p] = jnp.full((8, 128), PNO // 4 * numbers[3, p], jnp.int32)
    meta_ref[...] = meta.astype(F32)
    left = lax.broadcasted_iota(jnp.int32, (PNO, 128), 1) < NARROW

    def take(core):
        for o, copy in enumerate(copies):
            copy.wait()
            for k in range(CHIPS // 2):
                a = held[o, :, 256 * k : 256 * k + 128]
                b = held[o, :, 256 * k + 128 : 256 * k + 256]
                a, b = (a, pltpu.roll(b, NARROW, 1)) if core == 0 else (pltpu.roll(a, NARROW, 1), b)
                out_ref[o * PNO : (o + 1) * PNO, 128 * k : 128 * k + 128] = jnp.where(left, a, b)

    for core in range(2):
        pl.when(lax.axis_index("col") % 2 == core)(functools.partial(take, core))


def lagrangian_kernel(meta_ref, kept_ref, amp_ref, int_ref, keep_ref, up_ref, down_ref, held):
    far = jnp.maximum(
        lax.broadcasted_iota(jnp.int32, (PNO, PNO), 0), lax.broadcasted_iota(jnp.int32, (PNO, PNO), 1)
    )
    for p in range(SLOTS):
        kept = jnp.where(far < kept_ref[p, 0:1, :], amp_ref[0, p], 0.0)
        held[p] = dot3(split(kept), split(int_ref[0, p]), ((1,), (1,)))
    chip = lax.axis_index("col") // 2
    for ref, step, size in ((keep_ref, 0, HELD), (up_ref, 1, HELD), (down_ref, -1, FEWER)):
        for t in range(size // PART):
            start = pl.multiple_of((chip + step - 3 * t + CHIPS) % CHIPS * PART, PART)
            for p in range(SLOTS):
                at = p * size + t * PART
                ref[at : at + PART, :] = held[p, pl.ds(start, PART), :]
        ref[SLOTS * size :, :] = meta_ref[...]


def gather_kernel(keep_ref, below_ref, above_ref, block_ref):
    block_ref[...] = jnp.zeros_like(block_ref)
    for lag_ref, size in ((keep_ref, HELD), (below_ref, HELD), (above_ref, FEWER)):
        for p in range(SLOTS):
            number = lag_ref[SLOTS * size, p].astype(jnp.int32)
            block_ref[number, :size, :] += lag_ref[p * size : (p + 1) * size, :]


def arrived_kernel(second_ref, first_ref, second_out, first_out):
    pass


def images_kernel(mine_ref, other_ref, second_ref, own_ref, first_ref, out_ref):
    odd = (lax.axis_index("blk") + lax.axis_index("col") + 1) % 2
    size = ORB * HELD
    total = jnp.zeros((size, WIDE), F32)
    for start, x_ref in ((ORB, own_ref), (2 * ORB * odd, first_ref), (2 * ORB * (1 - odd), second_ref)):
        lhs = jnp.concatenate(
            [
                jnp.concatenate(
                    [mine_ref[(start + j) * ORB + o] + other_ref[(start + j) * ORB + o] for j in range(ORB)], axis=1
                )
                for o in range(ORB)
            ],
            axis=0,
        )
        hi, lo = split(lhs)
        x_hi, x_lo = split(x_ref[...])
        both = dot(jnp.concatenate([hi, lo]), x_hi)
        total += both[:size] + (both[size:] + dot(hi, x_lo))
    left = lax.broadcasted_iota(jnp.int32, (size // 2, 128), 1) < NARROW
    for k in range(CHIPS // 2):
        top = total[: size // 2, 128 * k : 128 * k + 128]
        low = total[size // 2 :, 128 * k : 128 * k + 128]
        out_ref[ORDER.index(2 * k)] = jnp.where(left, top, pltpu.roll(low, NARROW, 1))
        out_ref[ORDER.index(2 * k + 1)] = jnp.where(left, pltpu.roll(top, NARROW, 1), low)


def density_kernel(part_ref, coef_ref, out_ref, held, sems):
    sums = []
    for r in range(CHIPS):
        for o in range(2):
            a, b, c = (
                part_ref[ORDER.index((r + 3 * t) % CHIPS), o * HELD + t * PART : o * HELD + (t + 1) * PART, :]
                for t in range(3)
            )
            sums.append(a + b + c)
    sums = jnp.concatenate(sums, axis=0).T
    lhs = jnp.concatenate(split(jnp.concatenate([sums[:NARROW], sums[NARROW:]], axis=1)))
    copies = []
    for n in range(4):
        at = slice(256 * n, 256 * (n + 1))
        rhs = [
            coef_ref[2 * pair + o, r * PART : (r + 1) * PART, at]
            for pair in range(2)
            for r in range(CHIPS)
            for o in range(2)
        ]
        hi, lo = split(jnp.concatenate(rhs, axis=0))
        both = dot(lhs, hi)
        held[:, at] = both[:NARROW] + (both[NARROW:] + dot(lhs[:NARROW], lo))
        copies.append(pltpu.make_async_copy(held.at[:, at], out_ref.at[:, at], sems.at[n]))
        copies[-1].start()
    for copy in copies:
        copy.wait()


def cost(macs, size):
    return pl.CostEstimate(flops=2 * macs, bytes_accessed=size, transcendentals=0)


PARAMS = pltpu.CompilerParams(vmem_limit_bytes=48 * 1024 * 1024)


def local(pair_occ, pair_offset, pair_other, pno_blocks, pno_coef, amplitudes, integrals):
    tiles = lax.axis_size("blk")
    devices = lax.axis_size("col")
    in_place = lambda x: pltpu.with_memory_space_constraint(x, pltpu.HBM)

    own, numbers, kept = pl.pallas_call(
        select_kernel,
        in_specs=[pl.BlockSpec(memory_space=pltpu.HBM)] * 5,
        out_shape=(
            jax.ShapeDtypeStruct((ORB * PNO, WIDE), F32),
            jax.ShapeDtypeStruct((META, 128), F32),
            jax.ShapeDtypeStruct((SLOTS, 8, 128), jnp.int32),
        ),
        scratch_shapes=[
            pltpu.VMEM((ORB, PNO, AO), F32),
            pltpu.SMEM((4, SLOTS), jnp.int32),
            pltpu.SemaphoreType.DMA((ORB + 4,)),
        ],
        compiler_params=PARAMS,
        cost_estimate=cost(0, 3 << 20),
        name="select",
    )(*map(in_place, (pair_occ, pair_offset, pair_other, pno_blocks, pno_coef)))
    def halo(turn):
        pairs = []
        for b in range(tiles):
            for q in range(devices):
                there = (b + 2 * ((b + q + turn) % 2) - 1) % tiles
                pairs.append((b * devices + q, there * devices + q))
        return lax.ppermute(own, ("blk", "col"), pairs)

    second, first = halo(0), halo(1)

    pieces = lambda size: jax.ShapeDtypeStruct((SLOTS * size + META, 128), F32)
    keep, up, down = pl.pallas_call(
        lagrangian_kernel,
        out_shape=(pieces(HELD), pieces(HELD), pieces(FEWER)),
        scratch_shapes=[pltpu.VMEM((SLOTS, PNO, PNO), F32)],
        compiler_params=PARAMS,
        cost_estimate=cost(3 * SLOTS * PNO**3, 3 << 20),
        name="lagrangian",
    )(numbers, kept, amplitudes, integrals)

    shift = lambda x, chips: lax.ppermute(x, "col", [(i, (i + 2 * chips) % devices) for i in range(devices)])
    mine = pl.pallas_call(
        gather_kernel,
        out_shape=jax.ShapeDtypeStruct((TILES * ORB, HELD, PNO), F32),
        compiler_params=PARAMS,
        cost_estimate=cost(0, 0),
        name="gather",
    )(keep, shift(up, 1), shift(down, -1))
    other = lax.ppermute(mine, "col", [(i, i ^ 1) for i in range(devices)])

    anywhere = [pl.BlockSpec(memory_space=pl.ANY)] * 2
    second, first = pl.pallas_call(
        arrived_kernel,
        in_specs=anywhere,
        out_specs=anywhere,
        out_shape=(jax.ShapeDtypeStruct(own.shape, F32),) * 2,
        input_output_aliases={0: 0, 1: 1},
        compiler_params=PARAMS,
        cost_estimate=cost(ARRIVAL, 0),
        name="arrived",
    )(second, first)
    parts = pl.pallas_call(
        images_kernel,
        out_shape=jax.ShapeDtypeStruct((CHIPS, ORB * HELD // 2, 128), F32),
        compiler_params=PARAMS,
        cost_estimate=cost(3 * ORB * HELD * TILES * PNO * WIDE, 4 << 20),
        name="images",
    )(mine, other, second, own, first)
    groups = [[2 * z + c for z in ORDER] for c in range(2)]
    parts = lax.all_to_all(parts, "col", 0, 0, axis_index_groups=groups)

    out = pl.pallas_call(
        density_kernel,
        out_specs=pl.BlockSpec(memory_space=pl.ANY),
        out_shape=jax.ShapeDtypeStruct((NARROW, AO), F32),
        scratch_shapes=[pltpu.VMEM((NARROW, AO), F32), pltpu.SemaphoreType.DMA((4,))],
        compiler_params=PARAMS,
        cost_estimate=cost(3 * ORB * PNO * NARROW * AO, 3 << 20),
        name="density",
    )(parts, pno_coef)
    return out.T[None]


def solution(mesh):
    in_specs = (
        P("blk", "col"),
        P("blk", "col"),
        P("blk", "col"),
        P("blk", "col"),
        P("blk", None, None),
        P("blk", "col", None, None),
        P("blk", "col", None, None),
    )
    out_specs = P("blk", None, "col")
    return jax.shard_map(local, mesh=mesh, in_specs=in_specs, out_specs=out_specs, check_vma=False)
```

```python
import functools

import jax
import jax.numpy as jnp
from jax import lax
from jax.experimental import pallas as pl
from jax.experimental.pallas import tpu as pltpu
from jax.sharding import PartitionSpec as P

F32 = jnp.float32
BF16 = jnp.bfloat16
ORB = 4
PNO = 128
AO = 1024
SLOTS = 16
CHIPS = 8
WIDE = AO // 2
ORDER = (7, 4, 6, 5, 3, 2, 1, 0)
NARROW = AO // 16
PART = 16
HELD = 3 * PART
FEWER = 2 * PART
META = 8
TILES = 3 * ORB
ARRIVAL = 1 << 33


def split(x):
    hi = x.astype(BF16)
    return hi, (x - hi.astype(F32)).astype(BF16)


def dot(a, b, dims=((1,), (0,))):
    return lax.dot_general(a, b, (dims, ((), ())), preferred_element_type=F32)


def dot3(a, b, dims=((1,), (0,))):
    return dot(a[0], b[0], dims) + (dot(a[0], b[1], dims) + dot(a[1], b[0], dims))


def select_kernel(occ_ref, offset_ref, other_ref, blocks_ref, coef_ref, out_ref, meta_ref, keep_ref, held, numbers, sems):
    copies = [pltpu.make_async_copy(coef_ref.at[o], held.at[o], sems.at[o]) for o in range(ORB)]
    lists = [
        pltpu.make_async_copy(ref, numbers.at[pl.ds(i, 1)], sems.at[ORB + i])
        for i, ref in enumerate((occ_ref, offset_ref, other_ref, blocks_ref))
    ]
    for copy in copies + lists:
        copy.start()
    for copy in lists:
        copy.wait()
    lane = lax.broadcasted_iota(jnp.int32, (META, 128), 1)
    meta = jnp.zeros((META, 128), jnp.int32)
    for p in range(SLOTS):
        block = (numbers[1, p] * ORB + numbers[2, p]) * ORB + numbers[0, p]
        meta = jnp.where(lane == p, block, meta)
        keep_ref[p] = jnp.full((8, 128), PNO // 4 * numbers[3, p], jnp.int32)
    meta_ref[...] = meta.astype(F32)
    left = lax.broadcasted_iota(jnp.int32, (PNO, 128), 1) < NARROW

    def take(core):
        for o, copy in enumerate(copies):
            copy.wait()
            for k in range(CHIPS // 2):
                a = held[o, :, 256 * k : 256 * k + 128]
                b = held[o, :, 256 * k + 128 : 256 * k + 256]
                a, b = (a, pltpu.roll(b, NARROW, 1)) if core == 0 else (pltpu.roll(a, NARROW, 1), b)
                out_ref[o * PNO : (o + 1) * PNO, 128 * k : 128 * k + 128] = jnp.where(left, a, b)

    for core in range(2):
        pl.when(lax.axis_index("col") % 2 == core)(functools.partial(take, core))


def lagrangian_kernel(meta_ref, kept_ref, amp_ref, int_ref, keep_ref, up_ref, down_ref, held):
    far = jnp.maximum(
        lax.broadcasted_iota(jnp.int32, (PNO, PNO), 0), lax.broadcasted_iota(jnp.int32, (PNO, PNO), 1)
    )
    for p in range(SLOTS):
        kept = jnp.where(far < kept_ref[p, 0:1, :], amp_ref[0, p], 0.0)
        held[p] = dot3(split(kept), split(int_ref[0, p]), ((1,), (1,)))
    chip = lax.axis_index("col") // 2
    for ref, step, size in ((keep_ref, 0, HELD), (up_ref, 1, HELD), (down_ref, -1, FEWER)):
        for t in range(size // PART):
            start = pl.multiple_of((chip + step - 3 * t + CHIPS) % CHIPS * PART, PART)
            for p in range(SLOTS):
                at = p * size + t * PART
                ref[at : at + PART, :] = held[p, pl.ds(start, PART), :]
        ref[SLOTS * size :, :] = meta_ref[...]


def gather_kernel(keep_ref, below_ref, above_ref, block_ref):
    block_ref[...] = jnp.zeros_like(block_ref)
    for lag_ref, size in ((keep_ref, HELD), (below_ref, HELD), (above_ref, FEWER)):
        for p in range(SLOTS):
            number = lag_ref[SLOTS * size, p].astype(jnp.int32)
            block_ref[number, :size, :] += lag_ref[p * size : (p + 1) * size, :]


def arrived_kernel(second_ref, first_ref, second_out, first_out):
    pass


def images_kernel(mine_ref, other_ref, second_ref, own_ref, first_ref, out_ref):
    odd = (lax.axis_index("blk") + lax.axis_index("col") + 1) % 2
    size = ORB * HELD
    total = jnp.zeros((size, WIDE), F32)
    for start, x_ref in ((ORB, own_ref), (2 * ORB * odd, first_ref), (2 * ORB * (1 - odd), second_ref)):
        lhs = jnp.concatenate(
            [
                jnp.concatenate(
                    [mine_ref[(start + j) * ORB + o] + other_ref[(start + j) * ORB + o] for j in range(ORB)], axis=1
                )
                for o in range(ORB)
            ],
            axis=0,
        )
        hi, lo = split(lhs)
        x_hi, x_lo = split(x_ref[...])
        both = dot(jnp.concatenate([hi, lo]), x_hi)
        total += both[:size] + (both[size:] + dot(hi, x_lo))
    left = lax.broadcasted_iota(jnp.int32, (size // 2, 128), 1) < NARROW
    for k in range(CHIPS // 2):
        top = total[: size // 2, 128 * k : 128 * k + 128]
        low = total[size // 2 :, 128 * k : 128 * k + 128]
        out_ref[ORDER.index(2 * k)] = jnp.where(left, top, pltpu.roll(low, NARROW, 1))
        out_ref[ORDER.index(2 * k + 1)] = jnp.where(left, pltpu.roll(top, NARROW, 1), low)


def density_kernel(part_ref, coef_ref, out_ref, held, sems):
    sums = []
    for r in range(CHIPS):
        for o in range(2):
            a, b, c = (
                part_ref[ORDER.index((r + 3 * t) % CHIPS), o * HELD + t * PART : o * HELD + (t + 1) * PART, :]
                for t in range(3)
            )
            sums.append(a + b + c)
    sums = jnp.concatenate(sums, axis=0).T
    lhs = jnp.concatenate(split(jnp.concatenate([sums[:NARROW], sums[NARROW:]], axis=1)))
    copies = []
    for n in range(2):
        at = slice(512 * n, 512 * (n + 1))
        rhs = [
            coef_ref[2 * pair + o, r * PART : (r + 1) * PART, at]
            for pair in range(2)
            for r in range(CHIPS)
            for o in range(2)
        ]
        hi, lo = split(jnp.concatenate(rhs, axis=0))
        both = dot(lhs, hi)
        held[:, at] = both[:NARROW] + (both[NARROW:] + dot(lhs[:NARROW], lo))
        copies.append(pltpu.make_async_copy(held.at[:, at], out_ref.at[:, at], sems.at[n]))
        copies[-1].start()
    for copy in copies:
        copy.wait()


def cost(macs, size):
    return pl.CostEstimate(flops=2 * macs, bytes_accessed=size, transcendentals=0)


PARAMS = pltpu.CompilerParams(vmem_limit_bytes=48 * 1024 * 1024)


def local(pair_occ, pair_offset, pair_other, pno_blocks, pno_coef, amplitudes, integrals):
    tiles = lax.axis_size("blk")
    devices = lax.axis_size("col")
    in_place = lambda x: pltpu.with_memory_space_constraint(x, pltpu.HBM)

    own, numbers, kept = pl.pallas_call(
        select_kernel,
        in_specs=[pl.BlockSpec(memory_space=pltpu.HBM)] * 5,
        out_shape=(
            jax.ShapeDtypeStruct((ORB * PNO, WIDE), F32),
            jax.ShapeDtypeStruct((META, 128), F32),
            jax.ShapeDtypeStruct((SLOTS, 8, 128), jnp.int32),
        ),
        scratch_shapes=[
            pltpu.VMEM((ORB, PNO, AO), F32),
            pltpu.SMEM((4, SLOTS), jnp.int32),
            pltpu.SemaphoreType.DMA((ORB + 4,)),
        ],
        compiler_params=PARAMS,
        cost_estimate=cost(0, 3 << 20),
        name="select",
    )(*map(in_place, (pair_occ, pair_offset, pair_other, pno_blocks, pno_coef)))
    def halo(turn):
        pairs = []
        for b in range(tiles):
            for q in range(devices):
                there = (b + 2 * ((b + q + turn) % 2) - 1) % tiles
                pairs.append((b * devices + q, there * devices + q))
        return lax.ppermute(own, ("blk", "col"), pairs)

    second, first = halo(0), halo(1)

    pieces = lambda size: jax.ShapeDtypeStruct((SLOTS * size + META, 128), F32)
    keep, up, down = pl.pallas_call(
        lagrangian_kernel,
        out_shape=(pieces(HELD), pieces(HELD), pieces(FEWER)),
        scratch_shapes=[pltpu.VMEM((SLOTS, PNO, PNO), F32)],
        compiler_params=PARAMS,
        cost_estimate=cost(3 * SLOTS * PNO**3, 3 << 20),
        name="lagrangian",
    )(numbers, kept, amplitudes, integrals)

    shift = lambda x, chips: lax.ppermute(x, "col", [(i, (i + 2 * chips) % devices) for i in range(devices)])
    mine = pl.pallas_call(
        gather_kernel,
        out_shape=jax.ShapeDtypeStruct((TILES * ORB, HELD, PNO), F32),
        compiler_params=PARAMS,
        cost_estimate=cost(0, 0),
        name="gather",
    )(keep, shift(up, 1), shift(down, -1))
    other = lax.ppermute(mine, "col", [(i, i ^ 1) for i in range(devices)])

    anywhere = [pl.BlockSpec(memory_space=pl.ANY)] * 2
    second, first = pl.pallas_call(
        arrived_kernel,
        in_specs=anywhere,
        out_specs=anywhere,
        out_shape=(jax.ShapeDtypeStruct(own.shape, F32),) * 2,
        input_output_aliases={0: 0, 1: 1},
        compiler_params=PARAMS,
        cost_estimate=cost(ARRIVAL, 0),
        name="arrived",
    )(second, first)
    parts = pl.pallas_call(
        images_kernel,
        out_shape=jax.ShapeDtypeStruct((CHIPS, ORB * HELD // 2, 128), F32),
        compiler_params=PARAMS,
        cost_estimate=cost(3 * ORB * HELD * TILES * PNO * WIDE, 4 << 20),
        name="images",
    )(mine, other, second, own, first)
    groups = [[2 * z + c for z in ORDER] for c in range(2)]
    parts = lax.all_to_all(parts, "col", 0, 0, axis_index_groups=groups)

    out = pl.pallas_call(
        density_kernel,
        out_specs=pl.BlockSpec(memory_space=pl.ANY),
        out_shape=jax.ShapeDtypeStruct((NARROW, AO), F32),
        scratch_shapes=[pltpu.VMEM((NARROW, AO), F32), pltpu.SemaphoreType.DMA((2,))],
        compiler_params=PARAMS,
        cost_estimate=cost(3 * ORB * PNO * NARROW * AO, 3 << 20),
        name="density",
    )(parts, pno_coef)
    return out.T[None]


def solution(mesh):
    in_specs = (
        P("blk", "col"),
        P("blk", "col"),
        P("blk", "col"),
        P("blk", "col"),
        P("blk", None, None),
        P("blk", "col", None, None),
        P("blk", "col", None, None),
    )
    out_specs = P("blk", None, "col")
    return jax.shard_map(local, mesh=mesh, in_specs=in_specs, out_specs=out_specs, check_vma=False)
```
